768 devices in a mesh: rep: 96 (over z, y), tp: 8 (over x, core).
Axes of the slice: x: 4, y: 8, z: 12, core: 2. Of those that a mesh axis runs over, the one named last changes fastest.
Arguments:
- momentum: float32 [96, 128, 28672], P('rep', None, 'tp')
- grad: bfloat16 [96, 128, 28672], P('rep', None, 'tp'), may hold values from -6 to 6
- weight: float32 [128, 28672], P(None, 'tp'), may hold values from -6 to 6
- indices: int32 [96, 2, 14336], P(None, None, 'tp'), may hold values from 0 to 4095, as said below
Outputs:
- moment_out: float32 [96, 128, 28672], P('rep', None, 'tp')
- weight_out: float32 [128, 28672], P(None, 'tp')
The draws below stay inside these ranges and needn't reach their ends.
Inputs may be any that keep to these rules, and one draw needn't show every extreme that they name: `indices`: within each tile's 32 entries, the j-th lies in [j * 64 * 2, (j + 1) * 64 * 2), so they are distinct and rising.
All inputs are finite; a program needn't handle non-finite values.
Results may differ from the reference program's by a relative error of at most 0.0003.
Values sent between devices are 32-bit elements; how exact they have to be, the bound alone decides.
No kernel may reach another device: no remote copies, remote signals or barrier semaphores. Data moves between devices by JAX's collectives and lax.ppermute only.
A program may use at most 64 MiB of HBM per device.

```python
import jax
import jax.numpy as jnp
from jax import lax

FF = 28672
ROWS = 128
TILE = 64
TOPK = 32
N_REP = 96


def draw_momentum(key, part):
    key = jax.random.fold_in(key, 11)
    key_main, key_cols, key_rows = jax.random.split(key, 3)
    shape = (N_REP, ROWS, FF)
    ramp = 3.0 ** (jnp.arange(FF, dtype=jnp.float32) / FF)
    col_scale = ramp * jnp.exp(jax.random.uniform(key_cols, (FF,), jnp.float32, 0.0, jnp.log(10.0)))
    row_scale = jnp.exp(jax.random.uniform(key_rows, (ROWS, 1), jnp.float32, 0.0, jnp.log(10.0)))
    base = jax.random.normal(key_main, shape, jnp.float32)
    return (0.1 * base * col_scale[None, None, :] * row_scale[None]).astype(jnp.float32)


def draw_indices(key, part):
    key = jax.random.fold_in(key, 7)
    shape = (N_REP, ROWS // TILE, FF // TILE * TOPK)
    width = TILE * TILE // TOPK
    offset = jax.random.randint(key, shape, 0, width, dtype=jnp.int32)
    band = jnp.arange(shape[2], dtype=jnp.int32) % TOPK * width
    return offset + band[None, None, :]


def level_of(key, dims, shards, smallest, top_value):
    def one(axis_at, parts):
        draws = jax.random.uniform(jax.random.fold_in(jax.random.fold_in(key, 6), axis_at), (parts,), jnp.float32, smallest / len(shards), top_value / len(shards))
        return jnp.repeat(jnp.exp(draws), dims[axis_at] // parts).reshape((-1,) + (1,) * (len(dims) - axis_at - 1))

    loudness = one(*shards[0])
    for cut in shards[1:]:
        loudness = loudness * one(*cut)
    return loudness


def normal_values(rng, shape, spread, most, pieces=(), kind=jnp.bfloat16):
    result = jax.random.normal(rng, shape, jnp.float32) * spread
    if len(pieces) > 0:
        result = level_of(rng, shape, pieces, -0.22, 0.18) * result
    return jnp.clip(result, min=-most, max=most).astype(kind)


def setup_inputs(seed: int = 0) -> dict:
    streams_of = jax.random.split(jax.random.key(seed), 5)
    momentum = draw_momentum(jax.random.fold_in(streams_of[4], 71), 0)
    grad = normal_values(streams_of[1], (N_REP, ROWS, FF), 1.0, 6.0, ((0, 96), (2, 8)))
    weight = normal_values(streams_of[2], (ROWS, FF), 1.0, 6.0, ((1, 8),), jnp.float32)
    indices = draw_indices(jax.random.fold_in(streams_of[4], 71), 0)
    return {"momentum": momentum, "grad": grad, "weight": weight, "indices": indices}


BETA = 0.999
RATE = 0.25
EPS = 1e-06

def dct_table():
    freq = jnp.arange(TILE, dtype=jnp.float32)[:, None]
    place = jnp.arange(TILE, dtype=jnp.float32)[None, :]
    table = jnp.cos(jnp.pi * (2.0 * place + 1.0) * freq / (2.0 * TILE))
    factor = jnp.where(freq == 0, jnp.sqrt(1.0 / TILE), jnp.sqrt(2.0 / TILE))
    return (table * factor).astype(jnp.float32)

def forward(field, table):
    blocks = field.reshape(ROWS // TILE, TILE, FF // TILE, TILE)
    inner = jnp.einsum('ajbn,kn->ajbk', blocks, table, precision=lax.Precision.HIGHEST)
    return jnp.einsum('ij,ajbk->aibk', table, inner, precision=lax.Precision.HIGHEST)

def inverse(coeffs, table):
    inner = jnp.einsum('ij,aibk->ajbk', table, coeffs, precision=lax.Precision.HIGHEST)
    out = jnp.einsum('ajbk,kn->ajbn', inner, table, precision=lax.Precision.HIGHEST)
    return out.reshape(ROWS, FF)

def to_flat(coeffs):
    return coeffs.transpose(0, 2, 1, 3).reshape(ROWS // TILE, FF // TILE, TILE * TILE)

def from_flat(flat):
    return flat.reshape(ROWS // TILE, FF // TILE, TILE, TILE).transpose(0, 2, 1, 3)

def reference(momentum, grad, weight, indices):
    table = dct_table()
    tile_rows = ROWS // TILE
    tile_cols = FF // TILE
    chosen_all = indices.reshape(N_REP, tile_rows, tile_cols, TOPK)
    row_ix = jnp.arange(tile_rows, dtype=jnp.int32)[:, None, None]
    col_ix = jnp.arange(tile_cols, dtype=jnp.int32)[None, :, None]

    def step(summed, item):
        moment_row, grad_row, chosen = item
        decayed = BETA * moment_row + grad_row.astype(jnp.float32)
        flat = to_flat(forward(decayed, table))
        picked = jnp.take_along_axis(flat, chosen, axis=2)
        sparse = jnp.zeros((tile_rows, tile_cols, TILE * TILE), jnp.float32).at[row_ix, col_ix, chosen].add(picked)
        residual = decayed - inverse(from_flat(sparse), table)
        return (summed + sparse, residual)
    start = jnp.zeros((tile_rows, tile_cols, TILE * TILE), jnp.float32)
    summed, moment_out = lax.scan(step, start, (momentum, grad, chosen_all))
    decoded = inverse(from_flat(summed), table)
    scale = jnp.sqrt(jnp.mean(decoded * decoded) + EPS)
    weight_out = weight - RATE * decoded / scale
    return (moment_out, weight_out)
```

```python
import jax
import jax.numpy as jnp
import ml_dtypes
import numpy as np
from jax import lax
from jax.experimental import pallas as pl
from jax.experimental.pallas import tpu as pltpu
from jax.sharding import PartitionSpec as P

TILE = 64
TOPK = 32
BAND = TILE * TILE // TOPK
BETA = 0.999
RATE = 0.25
EPS = 1e-06

ROWS = 128
COLS = 3584
N_REP = 96
N_TP = 8
LANES = 128
GROUPS = 14
PAIRS = 2 * GROUPS
NONE = 127
VMEM = 60 << 20
HALVES = 2

Z, Y = 12, 8
ZR, YR = 3, 2
ZQ, YQ = Z // ZR, Y // YR


def far_groups():
    return [
        [(zq * ZR + zr) * Y + yq * YR + yr for zq in range(ZQ) for yq in range(YQ)]
        for zr in range(ZR)
        for yr in range(YR)
    ]


def near_groups():
    return [
        [(zq * ZR + zr) * Y + yq * YR + yr for zr in range(ZR) for yr in range(YR)]
        for zq in range(ZQ)
        for yq in range(YQ)
    ]


def replica_at():
    return [r for group in far_groups() for r in group]


def dct():
    k = np.arange(TILE, dtype=np.float64)[:, None]
    n = np.arange(TILE, dtype=np.float64)[None, :]
    c = np.where(k == 0, np.sqrt(1.0 / TILE), np.sqrt(2.0 / TILE))
    return c * np.cos(np.pi * (2 * n + 1) * k / (2 * TILE))


def two(x):
    x = np.asarray(x, np.float32)
    hi = x.astype(ml_dtypes.bfloat16)
    lo = (x - hi.astype(np.float32)).astype(ml_dtypes.bfloat16)
    return np.stack([hi, lo])


def split(x):
    hi = x.astype(jnp.bfloat16)
    return hi, (x - hi.astype(jnp.float32)).astype(jnp.bfloat16)


def mm(a, b):
    return jnp.dot(a, b, preferred_element_type=jnp.float32)


def times(x, table):
    hi, lo = split(x)
    return mm(hi, table[0]) + (mm(lo, table[0]) + mm(hi, table[1]))


def times_left(table, x):
    hi, lo = split(x)
    return mm(table[0], hi) + (mm(table[0], lo) + mm(table[1], hi))


def iota(shape, dim):
    return lax.broadcasted_iota(jnp.int32, shape, dim)


def stack(ref, n, width, axis=0):
    return jnp.concatenate([ref[:, width * g : width * g + width] for g in range(n)], axis=axis)


def kept_coefficients(momentum, grad, chosen, left, right, spread, wide):
    n = momentum.shape[2] // 256
    for g in range(n):
        c = slice(256 * g, 256 * g + 256)
        decayed = BETA * momentum[0, :, c] + grad[0, :, c].astype(jnp.float32)
        wide[ROWS * g : ROWS * g + ROWS, :] = decayed
    first = times(wide[...], right)
    row = iota((ROWS, LANES), 0)
    lane = iota((ROWS, LANES), 1)
    own = (row % TILE) // 2 == lane % TOPK
    base = (lane[:1] % TOPK) * BAND
    offsets = []
    for g in range(n):
        offset = chosen[0, :, LANES * g : LANES * g + LANES] - base
        per_row = jnp.where(row < TILE, offset[0:1], offset[1:2])
        offsets.append(jnp.where(own, per_row, 0).astype(jnp.float32).astype(jnp.bfloat16))
    offsets = mm(jnp.concatenate(offsets, axis=0), spread[...])
    row = iota((ROWS, 256), 0)
    lane = iota((ROWS, 256), 1)
    place = ((row % 2) * TILE + lane % TILE).astype(jnp.float32)
    for g in range(n):
        at = slice(ROWS * g, ROWS * g + ROWS)
        coeffs = times_left(left, first[at])
        wide[at, :] = jnp.where(offsets[at] == place, coeffs, 0.0)
    return own


def pick_kernel(rep, momentum, grad, chosen, left, right, spread, gather, out, wide):
    del rep
    own = kept_coefficients(momentum, grad, chosen, left, right, spread, wide)
    hi, lo = split(wide[...])
    both = mm(hi, gather[...]) + mm(lo, gather[...])
    for g in range(momentum.shape[2] // 256):
        block = jnp.where(own, both[ROWS * g : ROWS * g + ROWS], 0.0)
        top = jnp.sum(block[:TILE], axis=0, keepdims=True)
        low = jnp.sum(block[TILE:], axis=0, keepdims=True)
        value = jnp.concatenate([top, low], axis=0)
        for k in range(out.shape[0]):
            out[k, :, LANES * g : LANES * g + LANES] = value


def residual_kernel(rep, momentum, grad, chosen, left, right, spread, left_back, right_back, out, wide):
    del rep
    kept_coefficients(momentum, grad, chosen, left, right, spread, wide)
    n = momentum.shape[2] // 256
    for g in range(n):
        at = slice(ROWS * g, ROWS * g + ROWS)
        wide[at, :] = times_left(left_back, wide[at, :])
    back = times(wide[...], right_back)
    for g in range(n):
        c = slice(256 * g, 256 * g + 256)
        decayed = BETA * momentum[0, :, c] + grad[0, :, c].astype(jnp.float32)
        out[0, :, c] = decayed - back[ROWS * g : ROWS * g + ROWS]


def table_kernel(chosen, out, deep, rows):
    half = jnp.bfloat16
    order = replica_at()

    def one(step, carry):
        at = pl.multiple_of(step * LANES, LANES)
        base = (iota((N_REP, LANES), 1) % TOPK) * BAND
        rows[...] = (chosen[:, pl.ds(at, LANES)] - base).astype(jnp.float32)
        place = [(iota((16, LANES), 0) + 16 * v).astype(jnp.float32).astype(half) for v in range(BAND // 16)]
        none = jnp.full((16, LANES), NONE, half)
        first = [none] * (BAND // 16)
        after = [none] * (N_REP // 16)
        blocks = []
        for v in range(0, N_REP, 16):
            parts = [rows[pl.ds(order[v + q], YQ, stride=YR), :] for q in range(0, 16, YQ)]
            blocks.append(jnp.concatenate(parts, axis=0).astype(half))
        for p in reversed(range(N_REP)):
            row = jnp.broadcast_to(rows[order[p] : order[p] + 1, :], (16, LANES)).astype(half)
            me = jnp.full((16, LANES), p, half)
            for v in range(BAND // 16):
                first[v] = jnp.where(row == place[v], me, first[v])
            for v in range(p // 16 + 1):
                block = blocks[v]
                if v == p // 16:
                    block = jnp.where(place[0] < p % 16, block, jnp.full_like(block, -1))
                after[v] = jnp.where(row == block, me, after[v])
        after += [none] * ((LANES - N_REP) // 16)
        first = jnp.concatenate(first, axis=0).astype(jnp.float32).T.astype(jnp.int32)
        hop = jnp.concatenate(after, axis=0).astype(jnp.float32).T.astype(jnp.int32)
        hop2 = jnp.take_along_axis(hop, hop, axis=1)
        hop4 = jnp.take_along_axis(hop2, hop2, axis=1)
        hop8 = jnp.take_along_axis(hop4, hop4, axis=1)
        out[pl.ds(at, LANES), :] = hop | (hop2 << 7) | (hop4 << 14) | (first << 21)
        least = jnp.min(hop8.reshape(LANES // 8, 8, LANES), axis=0)
        deep[step] = jnp.where(jnp.min(least.astype(jnp.float32)) < NONE, 1, 0)
        return carry

    lax.fori_loop(0, chosen.shape[1] // LANES, one, 0)


def chain_sums(values, packed, levels):
    pad = jnp.zeros((LANES - N_REP, LANES), jnp.float32)
    total = jnp.concatenate([values, pad], axis=0).T
    for shift in (0, 7, 14):
        hop = (packed >> shift) & 127
        total = total + jnp.take_along_axis(total, hop, axis=1)
    for _ in range(levels):
        hop = jnp.take_along_axis(hop, hop, axis=1)
        total = total + jnp.take_along_axis(total, hop, axis=1)
    return jnp.take_along_axis(total, packed >> 21, axis=1)


def sum_kernel(top_deep, low_deep, values, top_table, low_table, out, energy, acc):
    step = pl.program_id(0)
    n = values.shape[1] // LANES
    upper = step < GROUPS // n

    @pl.when(step == 0)
    def _():
        acc[...] = jnp.zeros_like(acc)

    for s in range(n):
        at = slice(LANES * s, LANES * s + LANES)
        packed = jnp.where(upper, top_table[at, :], low_table[at, :])
        out[at, :] = chain_sums(values[:, at], packed, 0)

    def long_chains(s, carry):
        pair = step * n + s
        flag = jnp.where(upper, top_deep[jnp.minimum(pair, GROUPS - 1)], low_deep[jnp.maximum(pair - GROUPS, 0)])

        @pl.when(flag > 0)
        def _():
            at = pl.ds(pl.multiple_of(s * LANES, LANES), LANES)
            packed = jnp.where(upper, top_table[at, :], low_table[at, :])
            out[at, :] = chain_sums(values[:, at], packed, 4)

        return carry

    lax.fori_loop(0, n, long_chains, 0)
    summed = out[...]
    acc[...] += jnp.sum((summed * summed).reshape(LANES // 8 * n, 8, LANES), axis=0)

    @pl.when(step == pl.num_programs(0) - 1)
    def _():
        energy[...] = jnp.broadcast_to(acc[...][None], energy.shape)


def decode_kernel(summed, right, left, out, wide):
    wide[...] = times(summed[...], right)
    low = iota((TOPK, LANES), 1) < TILE
    for g in range(summed.shape[0] // LANES):
        pieces = []
        for u in (0, 2 * TOPK):
            a = slice(LANES * g + u, LANES * g + u + TOPK)
            b = slice(LANES * g + u + TOPK, LANES * g + u + 2 * TOPK)
            top = jnp.where(low, wide[a, :LANES], wide[b, LANES:])
            bottom = jnp.where(low, wide[a, LANES:], wide[b, :LANES])
            pieces.append(jnp.concatenate([top, bottom], axis=0))
        out[:, 256 * g : 256 * g + 256] = times_left(left, jnp.concatenate(pieces, axis=1))


def update_kernel(weight, decoded, energy, out):
    scale = jnp.sqrt(jnp.sum(energy[...]) / (ROWS * COLS * N_TP) + EPS)
    out[...] = weight[...] - decoded[...] * (RATE / jnp.full((1, 1), scale))


def whole(shape):
    return pl.BlockSpec(shape, lambda *_: (0,) * len(shape))


def params():
    return pltpu.CompilerParams(vmem_limit_bytes=VMEM)


def cost(flops, moved):
    return pl.CostEstimate(flops=flops, bytes_accessed=moved, transcendentals=0)


def constants():
    table = dct()
    eye2, eye4 = np.eye(2), np.eye(4)
    left = two(np.kron(eye2, table))
    right = two(np.kron(eye4, table.T))
    left_back = two(np.kron(eye2, table.T))
    right_back = two(np.kron(eye4, table))
    m = np.arange(LANES)[:, None]
    spread = (m // TOPK == np.arange(256)[None, :] // TILE).astype(ml_dtypes.bfloat16)
    pair = np.kron(eye2, table)
    cross = np.roll(pair, TILE, axis=1)
    decode_right = two(np.concatenate([pair, cross], axis=1))
    decode_left = two(np.concatenate([table[0::2], table[1::2]], axis=0).T)
    return left, right, left_back, right_back, spread, decode_right, decode_left


def own_specs():
    return [
        pl.BlockSpec((1, ROWS, COLS // HALVES), lambda g, rep: (0, 0, g)),
        pl.BlockSpec((1, ROWS, COLS // HALVES), lambda g, rep: (0, 0, g)),
        pl.BlockSpec((1, 2, COLS // HALVES // 2), lambda g, rep: (rep[0], 0, g)),
        whole((2, ROWS, ROWS)),
        whole((2, 256, 256)),
        whole((LANES, 256)),
    ]


def on_device(momentum, grad, weight, indices):
    left, right, left_back, right_back, spread, decode_right, decode_left = constants()
    rep = lax.axis_index("rep").astype(jnp.int32).reshape(1)
    picked = pl.pallas_call(
        pick_kernel,
        out_shape=jax.ShapeDtypeStruct((ZQ * YQ, 2, COLS // 2), jnp.float32),
        grid_spec=pltpu.PrefetchScalarGridSpec(
            num_scalar_prefetch=1,
            grid=(HALVES,),
            in_specs=own_specs() + [whole((256, LANES))],
            out_specs=pl.BlockSpec((ZQ * YQ, 2, COLS // HALVES // 2), lambda g, rep: (0, 0, g)),
            scratch_shapes=[pltpu.VMEM((ROWS * GROUPS // HALVES, 256), jnp.float32)],
        ),
        compiler_params=params(),
        cost_estimate=cost(1 << 30, 3 << 20),
    )(rep, momentum, grad, indices, left, right, spread, spread.T)

    far = lax.all_to_all(picked, "rep", 0, 0, tiled=True, axis_index_groups=far_groups())
    moment_out = pl.pallas_call(
        residual_kernel,
        out_shape=jax.ShapeDtypeStruct(momentum.shape, jnp.float32),
        grid_spec=pltpu.PrefetchScalarGridSpec(
            num_scalar_prefetch=1,
            grid=(HALVES,),
            in_specs=own_specs() + [whole((2, ROWS, ROWS)), whole((2, 256, 256))],
            out_specs=pl.BlockSpec((1, ROWS, COLS // HALVES), lambda g, rep: (0, 0, g)),
            scratch_shapes=[pltpu.VMEM((ROWS * GROUPS // HALVES, 256), jnp.float32)],
        ),
        compiler_params=params(),
        cost_estimate=cost(1 << 31, 5 << 20),
    )(rep, momentum, grad, indices, left, right, spread, left_back, right_back)

    flat = indices.reshape(N_REP, COLS)
    tables, deeps = [], []
    for a in range(2):
        table, deep = pl.pallas_call(
            table_kernel,
            out_shape=(
                jax.ShapeDtypeStruct((COLS // 2, LANES), jnp.int32),
                jax.ShapeDtypeStruct((GROUPS,), jnp.int32),
            ),
            grid=(1,),
            in_specs=[pl.BlockSpec((N_REP, COLS // 2), lambda s, a=a: (0, a))],
            out_specs=(
                pl.BlockSpec((COLS // 2, LANES), lambda s: (0, 0)),
                pl.BlockSpec(memory_space=pltpu.SMEM),
            ),
            scratch_shapes=[pltpu.VMEM((N_REP, LANES), jnp.float32)],
            compiler_params=params(),
            cost_estimate=cost(10 << 30, 2 << 20),
        )(flat)
        tables.append(table)
        deeps.append(deep)

    far, moment_out, tables[0] = lax.optimization_barrier((far, moment_out, tables[0]))
    near = jnp.broadcast_to(far.reshape(1, ZQ * YQ, COLS), (ZR * YR, ZQ * YQ, COLS))
    every = lax.all_to_all(near, "rep", 0, 0, tiled=True, axis_index_groups=near_groups())
    every = every.reshape(N_REP, COLS)

    wide = 7
    steps = PAIRS // wide
    half = steps // 2
    summed, energy = pl.pallas_call(
        sum_kernel,
        out_shape=(
            jax.ShapeDtypeStruct((COLS, LANES), jnp.float32),
            jax.ShapeDtypeStruct((N_TP, 8, LANES), jnp.float32),
        ),
        grid_spec=pltpu.PrefetchScalarGridSpec(
            num_scalar_prefetch=2,
            grid=(steps,),
            in_specs=[
                pl.BlockSpec((N_REP, wide * LANES), lambda s, *_: (0, s)),
                pl.BlockSpec((wide * LANES, LANES), lambda s, *_: (jnp.minimum(s, half - 1), 0)),
                pl.BlockSpec((wide * LANES, LANES), lambda s, *_: (jnp.maximum(s - half, 0), 0)),
            ],
            out_specs=(
                pl.BlockSpec((wide * LANES, LANES), lambda s, *_: (s, 0)),
                pl.BlockSpec((N_TP, 8, LANES), lambda s, *_: (0, 0, 0)),
            ),
            scratch_shapes=[pltpu.VMEM((8, LANES), jnp.float32)],
        ),
        compiler_params=params(),
        cost_estimate=cost(6 << 30, 5 << 20),
    )(*deeps, every, *tables)

    energies = lax.all_to_all(energy, "tp", 0, 0, tiled=True)

    decoded = pl.pallas_call(
        decode_kernel,
        out_shape=jax.ShapeDtypeStruct((ROWS, COLS), jnp.float32),
        grid=(2,),
        in_specs=[
            pl.BlockSpec((COLS // 2, LANES), lambda s: (s, 0)),
            whole((2, LANES, 256)),
            whole((2, TILE, TILE)),
        ],
        out_specs=pl.BlockSpec((TILE, COLS), lambda s: (s, 0)),
        scratch_shapes=[pltpu.VMEM((COLS // 2, 256), jnp.float32)],
        compiler_params=params(),
        cost_estimate=cost(1 << 30, 4 << 20),
    )(summed, decode_right, decode_left)

    weight_out = pl.pallas_call(
        update_kernel,
        out_shape=jax.ShapeDtypeStruct((ROWS, COLS), jnp.float32),
        grid=(2,),
        in_specs=[
            pl.BlockSpec((ROWS // 2, COLS), lambda s: (s, 0)),
            pl.BlockSpec((ROWS // 2, COLS), lambda s: (s, 0)),
            whole((N_TP, 8, LANES)),
        ],
        out_specs=pl.BlockSpec((ROWS // 2, COLS), lambda s: (s, 0)),
        compiler_params=params(),
        cost_estimate=cost(1 << 20, 6 << 20),
    )(weight, decoded, energies)
    return moment_out, weight_out


def solution(mesh):
    in_specs = (P("rep", None, "tp"), P("rep", None, "tp"), P(None, "tp"), P(None, None, "tp"))
    out_specs = (P("rep", None, "tp"), P(None, "tp"))
    return jax.shard_map(
        on_device, mesh=mesh, in_specs=in_specs, out_specs=out_specs, check_vma=False
    )
```

```python
import functools

import jax
import jax.numpy as jnp
import ml_dtypes
import numpy as np
from jax import lax
from jax.experimental import pallas as pl
from jax.experimental.pallas import tpu as pltpu
from jax.sharding import PartitionSpec as P

TILE = 64
TOPK = 32
BAND = TILE * TILE // TOPK
BETA = 0.999
RATE = 0.25
EPS = 1e-06

ROWS = 128
COLS = 3584
N_REP = 96
N_TP = 8
LANES = 128
GROUPS = 14
PAIRS = 2 * GROUPS
NONE = 127
VMEM = 60 << 20
HALVES = 2
CHUNK = 7
EARLY = 7

Z, Y = 12, 8
ZR, YR = 3, 2
ZQ, YQ = Z // ZR, Y // YR


def far_groups():
    return [
        [(zq * ZR + zr) * Y + yq * YR + yr for zq in range(ZQ) for yq in range(YQ)]
        for zr in range(ZR)
        for yr in range(YR)
    ]


def near_groups():
    return [
        [(zq * ZR + zr) * Y + yq * YR + yr for zr in range(ZR) for yr in range(YR)]
        for zq in range(ZQ)
        for yq in range(YQ)
    ]


def replica_at():
    return [r for group in far_groups() for r in group]


def dct():
    k = np.arange(TILE, dtype=np.float64)[:, None]
    n = np.arange(TILE, dtype=np.float64)[None, :]
    c = np.where(k == 0, np.sqrt(1.0 / TILE), np.sqrt(2.0 / TILE))
    return c * np.cos(np.pi * (2 * n + 1) * k / (2 * TILE))


def two(x):
    x = np.asarray(x, np.float32)
    hi = x.astype(ml_dtypes.bfloat16)
    lo = (x - hi.astype(np.float32)).astype(ml_dtypes.bfloat16)
    return np.stack([hi, lo])


def split(x):
    hi = x.astype(jnp.bfloat16)
    return hi, (x - hi.astype(jnp.float32)).astype(jnp.bfloat16)


def mm(a, b):
    return jnp.dot(a, b, preferred_element_type=jnp.float32)


def times(x, table):
    hi, lo = split(x)
    return mm(hi, table[0]) + (mm(lo, table[0]) + mm(hi, table[1]))


def times_left(table, x):
    hi, lo = split(x)
    return mm(table[0], hi) + (mm(table[0], lo) + mm(table[1], hi))


def iota(shape, dim):
    return lax.broadcasted_iota(jnp.int32, shape, dim)


def kept_coefficients(momentum, grad, chosen, left, right, spread, wide):
    n = momentum.shape[2] // 256
    for g in range(n):
        c = slice(256 * g, 256 * g + 256)
        decayed = BETA * momentum[0, :, c] + grad[0, :, c].astype(jnp.float32)
        wide[ROWS * g : ROWS * g + ROWS, :] = decayed
    first = times(wide[...], right)
    row = iota((ROWS, LANES), 0)
    lane = iota((ROWS, LANES), 1)
    own = (row % TILE) // 2 == lane % TOPK
    base = (lane[:1] % TOPK) * BAND
    offsets = []
    for g in range(n):
        offset = chosen[0, :, LANES * g : LANES * g + LANES] - base
        per_row = jnp.where(row < TILE, offset[0:1], offset[1:2])
        offsets.append(jnp.where(own, per_row, 0).astype(jnp.float32).astype(jnp.bfloat16))
    offsets = mm(jnp.concatenate(offsets, axis=0), spread[...])
    row = iota((ROWS, 256), 0)
    lane = iota((ROWS, 256), 1)
    place = ((row % 2) * TILE + lane % TILE).astype(jnp.float32)
    for g in range(n):
        at = slice(ROWS * g, ROWS * g + ROWS)
        coeffs = times_left(left, first[at])
        wide[at, :] = jnp.where(offsets[at] == place, coeffs, 0.0)
    return own


def pick_kernel(rep, momentum, grad, chosen, left, right, spread, gather, out, wide):
    del rep
    own = kept_coefficients(momentum, grad, chosen, left, right, spread, wide)
    hi, lo = split(wide[...])
    both = mm(hi, gather[...]) + mm(lo, gather[...])
    for g in range(momentum.shape[2] // 256):
        block = jnp.where(own, both[ROWS * g : ROWS * g + ROWS], 0.0)
        top = jnp.sum(block[:TILE], axis=0, keepdims=True)
        low = jnp.sum(block[TILE:], axis=0, keepdims=True)
        value = jnp.concatenate([top, low], axis=0)
        for k in range(out.shape[0]):
            out[k, :, LANES * g : LANES * g + LANES] = value


def residual_kernel(rep, momentum, grad, chosen, left, right, spread, left_back, right_back, out, wide):
    del rep
    kept_coefficients(momentum, grad, chosen, left, right, spread, wide)
    n = momentum.shape[2] // 256
    for g in range(n):
        at = slice(ROWS * g, ROWS * g + ROWS)
        wide[at, :] = times_left(left_back, wide[at, :])
    back = times(wide[...], right_back)
    for g in range(n):
        c = slice(256 * g, 256 * g + 256)
        decayed = BETA * momentum[0, :, c] + grad[0, :, c].astype(jnp.float32)
        out[0, :, c] = decayed - back[ROWS * g : ROWS * g + ROWS]


def table_kernel(start, count, indices, out, deep, rows, chosen, sem):
    columns = slice(start * LANES, (start + count) * LANES)
    load = pltpu.make_async_copy(indices.at[:, columns], chosen, sem)
    load.start()
    load.wait()
    half = jnp.bfloat16
    order = replica_at()

    def one(step, carry):
        at = pl.multiple_of(step * LANES, LANES)
        base = (iota((N_REP, LANES), 1) % TOPK) * BAND
        rows[...] = (chosen[:, pl.ds(at, LANES)] - base).astype(jnp.float32)
        place = [(iota((16, LANES), 0) + 16 * v).astype(jnp.float32).astype(half) for v in range(BAND // 16)]
        none = jnp.full((16, LANES), NONE, half)
        first = [none] * (BAND // 16)
        after = [none] * (N_REP // 16)
        blocks = []
        for v in range(0, N_REP, 16):
            parts = [rows[pl.ds(order[v + q], YQ, stride=YR), :] for q in range(0, 16, YQ)]
            blocks.append(jnp.concatenate(parts, axis=0).astype(half))
        for p in reversed(range(N_REP)):
            row = jnp.broadcast_to(rows[order[p] : order[p] + 1, :], (16, LANES)).astype(half)
            me = jnp.full((16, LANES), p, half)
            for v in range(BAND // 16):
                first[v] = jnp.where(row == place[v], me, first[v])
            for v in range(p // 16 + 1):
                block = blocks[v]
                if v == p // 16:
                    block = jnp.where(place[0] < p % 16, block, jnp.full_like(block, -1))
                after[v] = jnp.where(row == block, me, after[v])
        after += [none] * ((LANES - N_REP) // 16)
        first = jnp.concatenate(first, axis=0).astype(jnp.float32).T.astype(jnp.int32)
        hop = jnp.concatenate(after, axis=0).astype(jnp.float32).T.astype(jnp.int32)
        hop2 = jnp.take_along_axis(hop, hop, axis=1)
        hop4 = jnp.take_along_axis(hop2, hop2, axis=1)
        hop8 = jnp.take_along_axis(hop4, hop4, axis=1)
        out[pl.ds(at, LANES), :] = hop | (hop2 << 7) | (hop4 << 14) | (first << 21)
        least = jnp.min(hop8.reshape(LANES // 8, 8, LANES), axis=0)
        deep[step] = jnp.where(jnp.min(least.astype(jnp.float32)) < NONE, 1, 0)
        return carry

    lax.fori_loop(0, chosen.shape[1] // LANES, one, 0)


def chain_sums(values, packed, levels):
    pad = jnp.zeros((LANES - N_REP, LANES), jnp.float32)
    total = jnp.concatenate([values, pad], axis=0).T
    for shift in (0, 7, 14):
        hop = (packed >> shift) & 127
        total = total + jnp.take_along_axis(total, hop, axis=1)
    for _ in range(levels):
        hop = jnp.take_along_axis(hop, hop, axis=1)
        total = total + jnp.take_along_axis(total, hop, axis=1)
    return jnp.take_along_axis(total, packed >> 21, axis=1)


def sum_kernel(deep0, deep1, values, table0, table1, out, energy, acc):
    step = pl.program_id(0)
    early = step < EARLY // CHUNK

    @pl.when(step == 0)
    def _():
        acc[...] = jnp.zeros_like(acc)

    def run():
        total = jnp.zeros((8, LANES), jnp.float32)
        for s in range(CHUNK):
            at = slice(LANES * s, LANES * s + LANES)
            packed = jnp.where(early, table0[at, :], table1[at, :])
            summed = chain_sums(values[:, at], packed, 0)
            out[at, :] = summed
            total += jnp.sum((summed * summed).reshape(LANES // 8, 8, LANES), axis=0)
        acc[...] += total

    flag = jnp.int32(0)
    for s in range(CHUNK):
        pair = step * CHUNK + s
        late = deep1[jnp.maximum(pair - EARLY, 0)]
        flag = jnp.maximum(flag, jnp.where(early, deep0[jnp.minimum(pair, EARLY - 1)], late))

    @pl.when(flag == 0)
    def _():
        run()

    @pl.when(flag > 0)
    def _():
        before = acc[...]
        run()

        def long_chains(s, carry):
            pair = step * CHUNK + s
            late = deep1[jnp.maximum(pair - EARLY, 0)]

            @pl.when(jnp.where(early, deep0[jnp.minimum(pair, EARLY - 1)], late) > 0)
            def _():
                at = pl.ds(pl.multiple_of(s * LANES, LANES), LANES)
                packed = jnp.where(early, table0[at, :], table1[at, :])
                out[at, :] = chain_sums(values[:, at], packed, 4)

            return carry

        lax.fori_loop(0, CHUNK, long_chains, 0)
        summed = out[...]
        again = jnp.sum((summed * summed).reshape(LANES // 8 * CHUNK, 8, LANES), axis=0)
        acc[...] = before + again

    @pl.when(step == pl.num_programs(0) - 1)
    def _():
        energy[...] = jnp.broadcast_to(acc[...][None], energy.shape)


def decode_kernel(summed, right, left, out, wide):
    wide[...] = times(summed[...], right)
    low = iota((TOPK, LANES), 1) < TILE
    for g in range(summed.shape[0] // LANES):
        pieces = []
        for u in (0, 2 * TOPK):
            a = slice(LANES * g + u, LANES * g + u + TOPK)
            b = slice(LANES * g + u + TOPK, LANES * g + u + 2 * TOPK)
            top = jnp.where(low, wide[a, :LANES], wide[b, LANES:])
            bottom = jnp.where(low, wide[a, LANES:], wide[b, :LANES])
            pieces.append(jnp.concatenate([top, bottom], axis=0))
        out[:, 256 * g : 256 * g + 256] = times_left(left, jnp.concatenate(pieces, axis=1))


def update_kernel(weight, decoded, energy, out):
    scale = jnp.sqrt(jnp.sum(energy[...]) / (ROWS * COLS * N_TP) + EPS)
    out[...] = weight[...] - decoded[...] * (RATE / jnp.full((1, 1), scale))


def whole(shape):
    return pl.BlockSpec(shape, lambda *_: (0,) * len(shape))


def params(size=VMEM):
    return pltpu.CompilerParams(vmem_limit_bytes=size)


def cost(flops, moved):
    return pl.CostEstimate(flops=flops, bytes_accessed=moved, transcendentals=0)


def constants():
    table = dct()
    eye2, eye4 = np.eye(2), np.eye(4)
    left = two(np.kron(eye2, table))
    right = two(np.kron(eye4, table.T))
    left_back = two(np.kron(eye2, table.T))
    right_back = two(np.kron(eye4, table))
    m = np.arange(LANES)[:, None]
    spread = (m // TOPK == np.arange(256)[None, :] // TILE).astype(ml_dtypes.bfloat16)
    pair = np.kron(eye2, table)
    cross = np.roll(pair, TILE, axis=1)
    decode_right = two(np.concatenate([pair, cross], axis=1))
    decode_left = two(np.concatenate([table[0::2], table[1::2]], axis=0).T)
    return left, right, left_back, right_back, spread, decode_right, decode_left


def own_specs():
    return [
        pl.BlockSpec((1, ROWS, COLS // HALVES), lambda g, rep: (0, 0, g)),
        pl.BlockSpec((1, ROWS, COLS // HALVES), lambda g, rep: (0, 0, g)),
        pl.BlockSpec((1, 2, COLS // HALVES // 2), lambda g, rep: (rep[0], 0, g)),
        whole((2, ROWS, ROWS)),
        whole((2, 256, 256)),
        whole((LANES, 256)),
    ]


def on_device(momentum, grad, weight, indices):
    left, right, left_back, right_back, spread, decode_right, decode_left = constants()
    rep = lax.axis_index("rep").astype(jnp.int32).reshape(1)
    picked = pl.pallas_call(
        pick_kernel,
        out_shape=jax.ShapeDtypeStruct((ZQ * YQ, 2, COLS // 2), jnp.float32),
        grid_spec=pltpu.PrefetchScalarGridSpec(
            num_scalar_prefetch=1,
            grid=(HALVES,),
            in_specs=own_specs() + [whole((256, LANES))],
            out_specs=pl.BlockSpec((ZQ * YQ, 2, COLS // HALVES // 2), lambda g, rep: (0, 0, g)),
            scratch_shapes=[pltpu.VMEM((ROWS * GROUPS // HALVES, 256), jnp.float32)],
        ),
        compiler_params=params(),
        cost_estimate=cost(1 << 30, 3 << 20),
    )(rep, momentum, grad, indices, left, right, spread, spread.T)

    far = lax.all_to_all(picked, "rep", 0, 0, tiled=True, axis_index_groups=far_groups())
    moment_out = pl.pallas_call(
        residual_kernel,
        out_shape=jax.ShapeDtypeStruct(momentum.shape, jnp.float32),
        grid_spec=pltpu.PrefetchScalarGridSpec(
            num_scalar_prefetch=1,
            grid=(HALVES,),
            in_specs=own_specs() + [whole((2, ROWS, ROWS)), whole((2, 256, 256))],
            out_specs=pl.BlockSpec((1, ROWS, COLS // HALVES), lambda g, rep: (0, 0, g)),
            scratch_shapes=[pltpu.VMEM((ROWS * GROUPS // HALVES, 256), jnp.float32)],
        ),
        compiler_params=params(),
        cost_estimate=cost(1 << 31, 5 << 20),
    )(rep, momentum, grad, indices, left, right, spread, left_back, right_back)

    any_space = pl.BlockSpec(memory_space=pl.ANY)
    flat = indices.reshape(N_REP, COLS)
    tables, deeps = [], []
    for first, count in ((0, EARLY), (EARLY, PAIRS - EARLY)):
        table, deep = pl.pallas_call(
            functools.partial(table_kernel, first, count),
            out_shape=(
                jax.ShapeDtypeStruct((count * LANES, LANES), jnp.int32),
                jax.ShapeDtypeStruct((count,), jnp.int32),
            ),
            grid=(1,),
            in_specs=[any_space],
            out_specs=(
                pl.BlockSpec((count * LANES, LANES), lambda s: (0, 0)),
                pl.BlockSpec(memory_space=pltpu.SMEM),
            ),
            scratch_shapes=[
                pltpu.VMEM((N_REP, LANES), jnp.float32),
                pltpu.VMEM((N_REP, count * LANES), jnp.int32),
                pltpu.SemaphoreType.DMA,
            ],
            compiler_params=params(60 << 20),
            cost_estimate=cost(count << 30, 2 << 20),
        )(flat)
        tables.append(table)
        deeps.append(deep)

    far, moment_out, tables[0] = lax.optimization_barrier((far, moment_out, tables[0]))
    near = jnp.broadcast_to(far.reshape(1, ZQ * YQ, COLS), (ZR * YR, ZQ * YQ, COLS))
    every = lax.all_to_all(near, "rep", 0, 0, tiled=True, axis_index_groups=near_groups())
    every = every.reshape(N_REP, COLS)

    summed, energy = pl.pallas_call(
        sum_kernel,
        out_shape=(
            jax.ShapeDtypeStruct((COLS, LANES), jnp.float32),
            jax.ShapeDtypeStruct((N_TP, 8, LANES), jnp.float32),
        ),
        grid_spec=pltpu.PrefetchScalarGridSpec(
            num_scalar_prefetch=2,
            grid=(PAIRS // CHUNK,),
            in_specs=[
                pl.BlockSpec((N_REP, CHUNK * LANES), lambda s, *_: (0, s)),
                pl.BlockSpec((CHUNK * LANES, LANES), lambda s, *_: (jnp.minimum(s, EARLY // CHUNK - 1), 0)),
                pl.BlockSpec((CHUNK * LANES, LANES), lambda s, *_: (jnp.maximum(s - EARLY // CHUNK, 0), 0)),
            ],
            out_specs=(
                pl.BlockSpec((CHUNK * LANES, LANES), lambda s, *_: (s, 0)),
                whole((N_TP, 8, LANES)),
            ),
            scratch_shapes=[pltpu.VMEM((8, LANES), jnp.float32)],
        ),
        compiler_params=params(60 << 20),
        cost_estimate=cost(6 << 30, 5 << 20),
    )(*deeps, every, *tables)

    energies = lax.all_to_all(energy, "tp", 0, 0, tiled=True)

    decoded = pl.pallas_call(
        decode_kernel,
        out_shape=jax.ShapeDtypeStruct((ROWS, COLS), jnp.float32),
        grid=(2,),
        in_specs=[
            pl.BlockSpec((COLS // 2, LANES), lambda s: (s, 0)),
            whole((2, LANES, 256)),
            whole((2, TILE, TILE)),
        ],
        out_specs=pl.BlockSpec((TILE, COLS), lambda s: (s, 0)),
        scratch_shapes=[pltpu.VMEM((COLS // 2, 256), jnp.float32)],
        compiler_params=params(),
        cost_estimate=cost(1 << 30, 4 << 20),
    )(summed, decode_right, decode_left)

    weight_out = pl.pallas_call(
        update_kernel,
        out_shape=jax.ShapeDtypeStruct((ROWS, COLS), jnp.float32),
        grid=(2,),
        in_specs=[
            pl.BlockSpec((ROWS // 2, COLS), lambda s: (s, 0)),
            pl.BlockSpec((ROWS // 2, COLS), lambda s: (s, 0)),
            whole((N_TP, 8, LANES)),
        ],
        out_specs=pl.BlockSpec((ROWS // 2, COLS), lambda s: (s, 0)),
        compiler_params=params(),
        cost_estimate=cost(1 << 20, 6 << 20),
    )(weight, decoded, energies)
    return moment_out, weight_out


def solution(mesh):
    in_specs = (P("rep", None, "tp"), P("rep", None, "tp"), P(None, "tp"), P(None, None, "tp"))
    out_specs = (P("rep", None, "tp"), P(None, "tp"))
    return jax.shard_map(
        on_device, mesh=mesh, in_specs=in_specs, out_specs=out_specs, check_vma=False
    )
```

```python
import functools

import jax
import jax.numpy as jnp
import ml_dtypes
import numpy as np
from jax import lax
from jax.experimental import pallas as pl
from jax.experimental.pallas import tpu as pltpu
from jax.sharding import PartitionSpec as P

TILE = 64
TOPK = 32
BAND = TILE * TILE // TOPK
BETA = 0.999
RATE = 0.25
EPS = 1e-06

ROWS = 128
COLS = 3584
N_REP = 96
N_TP = 8
LANES = 128
GROUPS = 14
PAIRS = 2 * GROUPS
NONE = 127
VMEM = 60 << 20
HALVES = 2
CHUNK = 7
EARLY = 7

Z, Y = 12, 8
ZR, YR = 3, 2
ZQ, YQ = Z // ZR, Y // YR


def far_groups():
    return [
        [(zq * ZR + zr) * Y + yq * YR + yr for zq in range(ZQ) for yq in range(YQ)]
        for zr in range(ZR)
        for yr in range(YR)
    ]


def near_groups():
    return [
        [(zq * ZR + zr) * Y + yq * YR + yr for zr in range(ZR) for yr in range(YR)]
        for zq in range(ZQ)
        for yq in range(YQ)
    ]


def replica_at():
    return [r for group in far_groups() for r in group]


def dct():
    k = np.arange(TILE, dtype=np.float64)[:, None]
    n = np.arange(TILE, dtype=np.float64)[None, :]
    c = np.where(k == 0, np.sqrt(1.0 / TILE), np.sqrt(2.0 / TILE))
    return c * np.cos(np.pi * (2 * n + 1) * k / (2 * TILE))


def two(x):
    x = np.asarray(x, np.float32)
    hi = x.astype(ml_dtypes.bfloat16)
    lo = (x - hi.astype(np.float32)).astype(ml_dtypes.bfloat16)
    return np.stack([hi, lo])


def split(x):
    hi = x.astype(jnp.bfloat16)
    return hi, (x - hi.astype(jnp.float32)).astype(jnp.bfloat16)


def mm(a, b):
    return jnp.dot(a, b, preferred_element_type=jnp.float32)


def times(x, table):
    hi, lo = split(x)
    return mm(hi, table[0]) + (mm(lo, table[0]) + mm(hi, table[1]))


def times_left(table, x):
    hi, lo = split(x)
    return mm(table[0], hi) + (mm(table[0], lo) + mm(table[1], hi))


def iota(shape, dim):
    return lax.broadcasted_iota(jnp.int32, shape, dim)


def kept_coefficients(momentum, grad, chosen, left, right, spread, wide):
    n = momentum.shape[2] // 256
    for g in range(n):
        c = slice(256 * g, 256 * g + 256)
        decayed = BETA * momentum[0, :, c] + grad[0, :, c].astype(jnp.float32)
        wide[ROWS * g : ROWS * g + ROWS, :] = decayed
    first = times(wide[...], right)
    row = iota((ROWS, LANES), 0)
    lane = iota((ROWS, LANES), 1)
    own = (row % TILE) // 2 == lane % TOPK
    base = (lane[:1] % TOPK) * BAND
    offsets = []
    for g in range(n):
        offset = chosen[0, :, LANES * g : LANES * g + LANES] - base
        per_row = jnp.where(row < TILE, offset[0:1], offset[1:2])
        offsets.append(jnp.where(own, per_row, 0).astype(jnp.float32).astype(jnp.bfloat16))
    offsets = mm(jnp.concatenate(offsets, axis=0), spread[...])
    row = iota((ROWS, 256), 0)
    lane = iota((ROWS, 256), 1)
    place = ((row % 2) * TILE + lane % TILE).astype(jnp.float32)
    for g in range(n):
        at = slice(ROWS * g, ROWS * g + ROWS)
        coeffs = times_left(left, first[at])
        wide[at, :] = jnp.where(offsets[at] == place, coeffs, 0.0)
    return own


def pick_kernel(rep, momentum, grad, chosen, left, right, spread, gather, out, wide):
    del rep
    own = kept_coefficients(momentum, grad, chosen, left, right, spread, wide)
    hi, lo = split(wide[...])
    both = mm(hi, gather[...]) + mm(lo, gather[...])
    for g in range(momentum.shape[2] // 256):
        block = jnp.where(own, both[ROWS * g : ROWS * g + ROWS], 0.0)
        top = jnp.sum(block[:TILE], axis=0, keepdims=True)
        low = jnp.sum(block[TILE:], axis=0, keepdims=True)
        value = jnp.concatenate([top, low], axis=0)
        for k in range(out.shape[0]):
            out[k, :, LANES * g : LANES * g + LANES] = value


def residual_kernel(rep, momentum, grad, chosen, left, right, spread, left_back, right_back, out, wide):
    del rep
    kept_coefficients(momentum, grad, chosen, left, right, spread, wide)
    n = momentum.shape[2] // 256
    for g in range(n):
        at = slice(ROWS * g, ROWS * g + ROWS)
        wide[at, :] = times_left(left_back, wide[at, :])
    back = times(wide[...], right_back)
    for g in range(n):
        c = slice(256 * g, 256 * g + 256)
        decayed = BETA * momentum[0, :, c] + grad[0, :, c].astype(jnp.float32)
        out[0, :, c] = decayed - back[ROWS * g : ROWS * g + ROWS]


def table_kernel(start, count, indices, out, deep, rows, chosen, sem):
    columns = slice(start * LANES, (start + count) * LANES)
    load = pltpu.make_async_copy(indices.at[:, columns], chosen, sem)
    load.start()
    load.wait()
    half = jnp.bfloat16
    order = replica_at()

    def one(step, carry):
        at = pl.multiple_of(step * LANES, LANES)
        base = (iota((N_REP, LANES), 1) % TOPK) * BAND
        rows[...] = (chosen[:, pl.ds(at, LANES)] - base).astype(jnp.float32)
        place = [(iota((16, LANES), 0) + 16 * v).astype(jnp.float32).astype(half) for v in range(BAND // 16)]
        none = jnp.full((16, LANES), NONE, half)
        first = [none] * (BAND // 16)
        after = [none] * (N_REP // 16)
        blocks = []
        for v in range(0, N_REP, 16):
            parts = [rows[pl.ds(order[v + q], YQ, stride=YR), :] for q in range(0, 16, YQ)]
            blocks.append(jnp.concatenate(parts, axis=0).astype(half))
        for p in reversed(range(N_REP)):
            row = jnp.broadcast_to(rows[order[p] : order[p] + 1, :], (16, LANES)).astype(half)
            me = jnp.full((16, LANES), p, half)
            for v in range(BAND // 16):
                first[v] = jnp.where(row == place[v], me, first[v])
            for v in range(p // 16 + 1):
                block = blocks[v]
                if v == p // 16:
                    block = jnp.where(place[0] < p % 16, block, jnp.full_like(block, -1))
                after[v] = jnp.where(row == block, me, after[v])
        after += [none] * ((LANES - N_REP) // 16)
        first = jnp.concatenate(first, axis=0).astype(jnp.float32).T.astype(jnp.int32)
        hop = jnp.concatenate(after, axis=0).astype(jnp.float32).T.astype(jnp.int32)
        hop2 = jnp.take_along_axis(hop, hop, axis=1)
        hop4 = jnp.take_along_axis(hop2, hop2, axis=1)
        hop8 = jnp.take_along_axis(hop4, hop4, axis=1)
        out[pl.ds(at, LANES), :] = hop | (hop2 << 7) | (hop4 << 14) | (first << 21)
        least = jnp.min(hop8.reshape(LANES // 8, 8, LANES), axis=0)
        deep[step] = jnp.where(jnp.min(least.astype(jnp.float32)) < NONE, 1, 0)
        return carry

    lax.fori_loop(0, chosen.shape[1] // LANES, one, 0)


def chain_sums(values, packed, levels):
    pad = jnp.zeros((LANES - N_REP, LANES), jnp.float32)
    total = jnp.concatenate([values, pad], axis=0).T
    for shift in (0, 7, 14):
        hop = (packed >> shift) & 127
        total = total + jnp.take_along_axis(total, hop, axis=1)
    for _ in range(levels):
        hop = jnp.take_along_axis(hop, hop, axis=1)
        total = total + jnp.take_along_axis(total, hop, axis=1)
    return jnp.take_along_axis(total, packed >> 21, axis=1)


def sum_kernel(deep0, deep1, values, table0, table1, out, energy, acc):
    step = pl.program_id(0)
    early = step < EARLY // CHUNK

    @pl.when(step == 0)
    def _():
        acc[...] = jnp.zeros_like(acc)

    def run():
        total = jnp.zeros((8, LANES), jnp.float32)
        for s in range(CHUNK):
            at = slice(LANES * s, LANES * s + LANES)
            packed = jnp.where(early, table0[at, :], table1[at, :])
            summed = chain_sums(values[:, at], packed, 0)
            out[at, :] = summed
            total += jnp.sum((summed * summed).reshape(LANES // 8, 8, LANES), axis=0)
        acc[...] += total

    flag = jnp.int32(0)
    for s in range(CHUNK):
        pair = step * CHUNK + s
        late = deep1[jnp.maximum(pair - EARLY, 0)]
        flag = jnp.maximum(flag, jnp.where(early, deep0[jnp.minimum(pair, EARLY - 1)], late))

    @pl.when(flag == 0)
    def _():
        run()

    @pl.when(flag > 0)
    def _():
        before = acc[...]
        run()

        def long_chains(s, carry):
            pair = step * CHUNK + s
            late = deep1[jnp.maximum(pair - EARLY, 0)]

            @pl.when(jnp.where(early, deep0[jnp.minimum(pair, EARLY - 1)], late) > 0)
            def _():
                at = pl.ds(pl.multiple_of(s * LANES, LANES), LANES)
                packed = jnp.where(early, table0[at, :], table1[at, :])
                out[at, :] = chain_sums(values[:, at], packed, 4)

            return carry

        lax.fori_loop(0, CHUNK, long_chains, 0)
        summed = out[...]
        again = jnp.sum((summed * summed).reshape(LANES // 8 * CHUNK, 8, LANES), axis=0)
        acc[...] = before + again

    @pl.when(step == pl.num_programs(0) - 1)
    def _():
        energy[...] = jnp.broadcast_to(acc[...][None], energy.shape)


def decode_kernel(summed, right, left, out, wide):
    wide[...] = times(summed[...], right)
    low = iota((TOPK, LANES), 1) < TILE
    for g in range(summed.shape[0] // LANES):
        pieces = []
        for u in (0, 2 * TOPK):
            a = slice(LANES * g + u, LANES * g + u + TOPK)
            b = slice(LANES * g + u + TOPK, LANES * g + u + 2 * TOPK)
            top = jnp.where(low, wide[a, :LANES], wide[b, LANES:])
            bottom = jnp.where(low, wide[a, LANES:], wide[b, :LANES])
            pieces.append(jnp.concatenate([top, bottom], axis=0))
        out[:, 256 * g : 256 * g + 256] = times_left(left, jnp.concatenate(pieces, axis=1))


def update_kernel(weight, decoded, energy, out):
    scale = jnp.sqrt(jnp.sum(energy[...]) / (ROWS * COLS * N_TP) + EPS)
    out[...] = weight[...] - decoded[...] * (RATE / jnp.full((1, 1), scale))


def whole(shape):
    return pl.BlockSpec(shape, lambda *_: (0,) * len(shape))


def params(size=VMEM):
    return pltpu.CompilerParams(vmem_limit_bytes=size)


def cost(flops, moved):
    return pl.CostEstimate(flops=flops, bytes_accessed=moved, transcendentals=0)


def constants():
    table = dct()
    eye2, eye4 = np.eye(2), np.eye(4)
    left = two(np.kron(eye2, table))
    right = two(np.kron(eye4, table.T))
    left_back = two(np.kron(eye2, table.T))
    right_back = two(np.kron(eye4, table))
    m = np.arange(LANES)[:, None]
    spread = (m // TOPK == np.arange(256)[None, :] // TILE).astype(ml_dtypes.bfloat16)
    pair = np.kron(eye2, table)
    cross = np.roll(pair, TILE, axis=1)
    decode_right = two(np.concatenate([pair, cross], axis=1))
    decode_left = two(np.concatenate([table[0::2], table[1::2]], axis=0).T)
    return left, right, left_back, right_back, spread, decode_right, decode_left


def own_specs():
    return [
        pl.BlockSpec((1, ROWS, COLS // HALVES), lambda g, rep: (0, 0, g)),
        pl.BlockSpec((1, ROWS, COLS // HALVES), lambda g, rep: (0, 0, g)),
        pl.BlockSpec((1, 2, COLS // HALVES // 2), lambda g, rep: (rep[0], 0, g)),
        whole((2, ROWS, ROWS)),
        whole((2, 256, 256)),
        whole((LANES, 256)),
    ]


def on_device(momentum, grad, weight, indices):
    left, right, left_back, right_back, spread, decode_right, decode_left = constants()
    rep = lax.axis_index("rep").astype(jnp.int32).reshape(1)
    picked = pl.pallas_call(
        pick_kernel,
        out_shape=jax.ShapeDtypeStruct((ZQ * YQ, 2, COLS // 2), jnp.float32),
        grid_spec=pltpu.PrefetchScalarGridSpec(
            num_scalar_prefetch=1,
            grid=(HALVES,),
            in_specs=own_specs() + [whole((256, LANES))],
            out_specs=pl.BlockSpec((ZQ * YQ, 2, COLS // HALVES // 2), lambda g, rep: (0, 0, g)),
            scratch_shapes=[pltpu.VMEM((ROWS * GROUPS // HALVES, 256), jnp.float32)],
        ),
        compiler_params=params(),
        cost_estimate=cost(1 << 30, 3 << 20),
    )(rep, momentum, grad, indices, left, right, spread, spread.T)

    far = lax.all_to_all(picked, "rep", 0, 0, tiled=True, axis_index_groups=far_groups())
    moment_out = pl.pallas_call(
        residual_kernel,
        out_shape=jax.ShapeDtypeStruct(momentum.shape, jnp.float32),
        grid_spec=pltpu.PrefetchScalarGridSpec(
            num_scalar_prefetch=1,
            grid=(HALVES,),
            in_specs=own_specs() + [whole((2, ROWS, ROWS)), whole((2, 256, 256))],
            out_specs=pl.BlockSpec((1, ROWS, COLS // HALVES), lambda g, rep: (0, 0, g)),
            scratch_shapes=[pltpu.VMEM((ROWS * GROUPS // HALVES, 256), jnp.float32)],
        ),
        compiler_params=params(),
        cost_estimate=cost(1 << 31, 5 << 20),
    )(rep, momentum, grad, indices, left, right, spread, left_back, right_back)

    any_space = pl.BlockSpec(memory_space=pl.ANY)
    flat = indices.reshape(N_REP, COLS)
    tables, deeps = [], []
    for first, count in ((0, EARLY), (EARLY, PAIRS - EARLY)):
        table, deep = pl.pallas_call(
            functools.partial(table_kernel, first, count),
            out_shape=(
                jax.ShapeDtypeStruct((count * LANES, LANES), jnp.int32),
                jax.ShapeDtypeStruct((count,), jnp.int32),
            ),
            grid=(1,),
            in_specs=[any_space],
            out_specs=(
                pl.BlockSpec((count * LANES, LANES), lambda s: (0, 0)),
                pl.BlockSpec(memory_space=pltpu.SMEM),
            ),
            scratch_shapes=[
                pltpu.VMEM((N_REP, LANES), jnp.float32),
                pltpu.VMEM((N_REP, count * LANES), jnp.int32),
                pltpu.SemaphoreType.DMA,
            ],
            compiler_params=params(60 << 20),
            cost_estimate=cost(count << 30, 2 << 20),
        )(flat)
        tables.append(table)
        deeps.append(deep)

    far, moment_out, tables[0] = lax.optimization_barrier((far, moment_out, tables[0]))
    near = jnp.broadcast_to(far.reshape(1, ZQ * YQ, COLS), (ZR * YR, ZQ * YQ, COLS))
    every = lax.all_to_all(near, "rep", 0, 0, tiled=True, axis_index_groups=near_groups())
    every = every.reshape(N_REP, COLS)

    summed, energy = pl.pallas_call(
        sum_kernel,
        out_shape=(
            pltpu.HBM((COLS, LANES), jnp.float32),
            jax.ShapeDtypeStruct((N_TP, 8, LANES), jnp.float32),
        ),
        grid_spec=pltpu.PrefetchScalarGridSpec(
            num_scalar_prefetch=2,
            grid=(PAIRS // CHUNK,),
            in_specs=[
                pl.BlockSpec((N_REP, CHUNK * LANES), lambda s, *_: (0, s)),
                pl.BlockSpec((CHUNK * LANES, LANES), lambda s, *_: (jnp.minimum(s, EARLY // CHUNK - 1), 0)),
                pl.BlockSpec((CHUNK * LANES, LANES), lambda s, *_: (jnp.maximum(s - EARLY // CHUNK, 0), 0)),
            ],
            out_specs=(
                pl.BlockSpec((CHUNK * LANES, LANES), lambda s, *_: (s, 0)),
                whole((N_TP, 8, LANES)),
            ),
            scratch_shapes=[pltpu.VMEM((8, LANES), jnp.float32)],
        ),
        compiler_params=params(40 << 20),
        cost_estimate=cost(6 << 30, 5 << 20),
    )(*deeps, every, *tables)

    energies = lax.all_to_all(energy, "tp", 0, 0, tiled=True)

    decoded = pl.pallas_call(
        decode_kernel,
        out_shape=jax.ShapeDtypeStruct((ROWS, COLS), jnp.float32),
        grid=(2,),
        in_specs=[
            pl.BlockSpec((COLS // 2, LANES), lambda s: (s, 0)),
            whole((2, LANES, 256)),
            whole((2, TILE, TILE)),
        ],
        out_specs=pl.BlockSpec((TILE, COLS), lambda s: (s, 0)),
        scratch_shapes=[pltpu.VMEM((COLS // 2, 256), jnp.float32)],
        compiler_params=params(),
        cost_estimate=cost(1 << 30, 4 << 20),
    )(summed, decode_right, decode_left)

    weight_out = pl.pallas_call(
        update_kernel,
        out_shape=jax.ShapeDtypeStruct((ROWS, COLS), jnp.float32),
        grid=(2,),
        in_specs=[
            pl.BlockSpec((ROWS // 2, COLS), lambda s: (s, 0)),
            pl.BlockSpec((ROWS // 2, COLS), lambda s: (s, 0)),
            whole((N_TP, 8, LANES)),
        ],
        out_specs=pl.BlockSpec((ROWS // 2, COLS), lambda s: (s, 0)),
        compiler_params=params(),
        cost_estimate=cost(1 << 20, 6 << 20),
    )(weight, decoded, energies)
    return moment_out, weight_out


def solution(mesh):
    in_specs = (P("rep", None, "tp"), P("rep", None, "tp"), P(None, "tp"), P(None, None, "tp"))
    out_specs = (P("rep", None, "tp"), P(None, "tp"))
    return jax.shard_map(
        on_device, mesh=mesh, in_specs=in_specs, out_specs=out_specs, check_vma=False
    )
```

```python
import functools

import jax
import jax.numpy as jnp
import ml_dtypes
import numpy as np
from jax import lax
from jax.experimental import pallas as pl
from jax.experimental.pallas import tpu as pltpu
from jax.sharding import PartitionSpec as P

TILE = 64
TOPK = 32
BAND = TILE * TILE // TOPK
BETA = 0.999
RATE = 0.25
EPS = 1e-06

ROWS = 128
COLS = 3584
N_REP = 96
N_TP = 8
LANES = 128
GROUPS = 14
PAIRS = 2 * GROUPS
NONE = 127
VMEM = 60 << 20
HALVES = 2
CHUNK = 7
EARLY = 7

Z, Y = 12, 8
ZR, YR = 3, 2
ZQ, YQ = Z // ZR, Y // YR


def far_groups():
    return [
        [(zq * ZR + zr) * Y + yq * YR + yr for zq in range(ZQ) for yq in range(YQ)]
        for zr in range(ZR)
        for yr in range(YR)
    ]


def near_groups():
    return [
        [(zq * ZR + zr) * Y + yq * YR + yr for zr in range(ZR) for yr in range(YR)]
        for zq in range(ZQ)
        for yq in range(YQ)
    ]


def replica_at():
    return [r for group in far_groups() for r in group]


def dct():
    k = np.arange(TILE, dtype=np.float64)[:, None]
    n = np.arange(TILE, dtype=np.float64)[None, :]
    c = np.where(k == 0, np.sqrt(1.0 / TILE), np.sqrt(2.0 / TILE))
    return c * np.cos(np.pi * (2 * n + 1) * k / (2 * TILE))


def two(x):
    x = np.asarray(x, np.float32)
    hi = x.astype(ml_dtypes.bfloat16)
    lo = (x - hi.astype(np.float32)).astype(ml_dtypes.bfloat16)
    return np.stack([hi, lo])


def split(x):
    hi = x.astype(jnp.bfloat16)
    return hi, (x - hi.astype(jnp.float32)).astype(jnp.bfloat16)


def mm(a, b):
    return jnp.dot(a, b, preferred_element_type=jnp.float32)


def times(x, table):
    hi, lo = split(x)
    return mm(hi, table[0]) + (mm(lo, table[0]) + mm(hi, table[1]))


def times_left(table, x):
    hi, lo = split(x)
    return mm(table[0], hi) + (mm(table[0], lo) + mm(table[1], hi))


def iota(shape, dim):
    return lax.broadcasted_iota(jnp.int32, shape, dim)


def kept_coefficients(momentum, grad, chosen, left, right, spread, wide):
    n = momentum.shape[2] // 256
    for g in range(n):
        c = slice(256 * g, 256 * g + 256)
        decayed = BETA * momentum[0, :, c] + grad[0, :, c].astype(jnp.float32)
        wide[ROWS * g : ROWS * g + ROWS, :] = decayed
    first = times(wide[...], right)
    row = iota((ROWS, LANES), 0)
    lane = iota((ROWS, LANES), 1)
    own = (row % TILE) // 2 == lane % TOPK
    base = (lane[:1] % TOPK) * BAND
    offsets = []
    for g in range(n):
        offset = chosen[0, :, LANES * g : LANES * g + LANES] - base
        per_row = jnp.where(row < TILE, offset[0:1], offset[1:2])
        offsets.append(jnp.where(own, per_row, 0).astype(jnp.float32).astype(jnp.bfloat16))
    offsets = mm(jnp.concatenate(offsets, axis=0), spread[...])
    row = iota((ROWS, 256), 0)
    lane = iota((ROWS, 256), 1)
    place = ((row % 2) * TILE + lane % TILE).astype(jnp.float32)
    for g in range(n):
        at = slice(ROWS * g, ROWS * g + ROWS)
        coeffs = times_left(left, first[at])
        wide[at, :] = jnp.where(offsets[at] == place, coeffs, 0.0)
    return own


def pick_kernel(rep, momentum, grad, chosen, left, right, spread, gather, out, wide):
    del rep
    own = kept_coefficients(momentum, grad, chosen, left, right, spread, wide)
    hi, lo = split(wide[...])
    both = mm(hi, gather[...]) + mm(lo, gather[...])
    for g in range(momentum.shape[2] // 256):
        block = jnp.where(own, both[ROWS * g : ROWS * g + ROWS], 0.0)
        top = jnp.sum(block[:TILE], axis=0, keepdims=True)
        low = jnp.sum(block[TILE:], axis=0, keepdims=True)
        value = jnp.concatenate([top, low], axis=0)
        for k in range(out.shape[0]):
            out[k, :, LANES * g : LANES * g + LANES] = value


def residual_kernel(rep, momentum, grad, chosen, left, right, spread, left_back, right_back, out, wide):
    del rep
    kept_coefficients(momentum, grad, chosen, left, right, spread, wide)
    n = momentum.shape[2] // 256
    for g in range(n):
        at = slice(ROWS * g, ROWS * g + ROWS)
        wide[at, :] = times_left(left_back, wide[at, :])
    back = times(wide[...], right_back)
    for g in range(n):
        c = slice(256 * g, 256 * g + 256)
        decayed = BETA * momentum[0, :, c] + grad[0, :, c].astype(jnp.float32)
        out[0, :, c] = decayed - back[ROWS * g : ROWS * g + ROWS]


def table_kernel(start, count, indices, out, deep, rows, chosen, sem):
    columns = slice(start * LANES, (start + count) * LANES)
    load = pltpu.make_async_copy(indices.at[:, columns], chosen, sem)
    load.start()
    load.wait()
    half = jnp.bfloat16
    order = replica_at()

    def one(step, carry):
        at = pl.multiple_of(step * LANES, LANES)
        base = (iota((N_REP, LANES), 1) % TOPK) * BAND
        rows[...] = (chosen[:, pl.ds(at, LANES)] - base).astype(jnp.float32)
        place = [(iota((16, LANES), 0) + 16 * v).astype(jnp.float32).astype(half) for v in range(BAND // 16)]
        none = jnp.full((16, LANES), NONE, half)
        first = [none] * (BAND // 16)
        after = [none] * (N_REP // 16)
        blocks = []
        for v in range(0, N_REP, 16):
            parts = [rows[pl.ds(order[v + q], YQ, stride=YR), :] for q in range(0, 16, YQ)]
            blocks.append(jnp.concatenate(parts, axis=0).astype(half))
        for p in reversed(range(N_REP)):
            row = jnp.broadcast_to(rows[order[p] : order[p] + 1, :], (16, LANES)).astype(half)
            me = jnp.full((16, LANES), p, half)
            for v in range(BAND // 16):
                first[v] = jnp.where(row == place[v], me, first[v])
            for v in range(p // 16 + 1):
                block = blocks[v]
                if v == p // 16:
                    block = jnp.where(place[0] < p % 16, block, jnp.full_like(block, -1))
                after[v] = jnp.where(row == block, me, after[v])
        after += [none] * ((LANES - N_REP) // 16)
        first = jnp.concatenate(first, axis=0).astype(jnp.float32).T.astype(jnp.int32)
        hop = jnp.concatenate(after, axis=0).astype(jnp.float32).T.astype(jnp.int32)
        hop2 = jnp.take_along_axis(hop, hop, axis=1)
        hop4 = jnp.take_along_axis(hop2, hop2, axis=1)
        hop8 = jnp.take_along_axis(hop4, hop4, axis=1)
        out[pl.ds(at, LANES), :] = hop | (hop2 << 7) | (hop4 << 14) | (first << 21)
        least = jnp.min(hop8.reshape(LANES // 8, 8, LANES), axis=0)
        deep[step] = jnp.where(jnp.min(least.astype(jnp.float32)) < NONE, 1, 0)
        return carry

    lax.fori_loop(0, chosen.shape[1] // LANES, one, 0)


def chain_sums(values, packed, levels):
    pad = jnp.zeros((LANES - N_REP, LANES), jnp.float32)
    total = jnp.concatenate([values, pad], axis=0).T
    for shift in (0, 7, 14):
        hop = (packed >> shift) & 127
        total = total + jnp.take_along_axis(total, hop, axis=1)
    for _ in range(levels):
        hop = jnp.take_along_axis(hop, hop, axis=1)
        total = total + jnp.take_along_axis(total, hop, axis=1)
    return jnp.take_along_axis(total, packed >> 21, axis=1)


def sum_kernel(deep0, deep1, values, table0, table1, out, energy, acc):
    step = pl.program_id(0)
    early = step < EARLY // CHUNK

    @pl.when(step == 0)
    def _():
        acc[...] = jnp.zeros_like(acc)

    def run():
        total = jnp.zeros((8, LANES), jnp.float32)
        for s in range(CHUNK):
            at = slice(LANES * s, LANES * s + LANES)
            packed = jnp.where(early, table0[at, :], table1[at, :])
            summed = chain_sums(values[:, at], packed, 0)
            out[at, :] = summed
            total += jnp.sum((summed * summed).reshape(LANES // 8, 8, LANES), axis=0)
        acc[...] += total

    flag = jnp.int32(0)
    for s in range(CHUNK):
        pair = step * CHUNK + s
        late = deep1[jnp.maximum(pair - EARLY, 0)]
        flag = jnp.maximum(flag, jnp.where(early, deep0[jnp.minimum(pair, EARLY - 1)], late))

    @pl.when(flag == 0)
    def _():
        run()

    @pl.when(flag > 0)
    def _():
        before = acc[...]
        run()

        def long_chains(s, carry):
            pair = step * CHUNK + s
            late = deep1[jnp.maximum(pair - EARLY, 0)]

            @pl.when(jnp.where(early, deep0[jnp.minimum(pair, EARLY - 1)], late) > 0)
            def _():
                at = pl.ds(pl.multiple_of(s * LANES, LANES), LANES)
                packed = jnp.where(early, table0[at, :], table1[at, :])
                out[at, :] = chain_sums(values[:, at], packed, 4)

            return carry

        lax.fori_loop(0, CHUNK, long_chains, 0)
        summed = out[...]
        again = jnp.sum((summed * summed).reshape(LANES // 8 * CHUNK, 8, LANES), axis=0)
        acc[...] = before + again

    @pl.when(step == pl.num_programs(0) - 1)
    def _():
        energy[...] = jnp.broadcast_to(acc[...][None], energy.shape)


def decode_kernel(summed, right, left, out, wide):
    wide[...] = times(summed[...], right)
    low = iota((TOPK, LANES), 1) < TILE
    for g in range(summed.shape[0] // LANES):
        pieces = []
        for u in (0, 2 * TOPK):
            a = slice(LANES * g + u, LANES * g + u + TOPK)
            b = slice(LANES * g + u + TOPK, LANES * g + u + 2 * TOPK)
            top = jnp.where(low, wide[a, :LANES], wide[b, LANES:])
            bottom = jnp.where(low, wide[a, LANES:], wide[b, :LANES])
            pieces.append(jnp.concatenate([top, bottom], axis=0))
        out[:, 256 * g : 256 * g + 256] = times_left(left, jnp.concatenate(pieces, axis=1))


def update_kernel(weight, decoded, energy, out):
    scale = jnp.sqrt(jnp.sum(energy[...]) / (ROWS * COLS * N_TP) + EPS)
    out[...] = weight[...] - decoded[...] * (RATE / jnp.full((1, 1), scale))


def whole(shape):
    return pl.BlockSpec(shape, lambda *_: (0,) * len(shape))


def params(size=VMEM):
    return pltpu.CompilerParams(vmem_limit_bytes=size)


def cost(flops, moved):
    return pl.CostEstimate(flops=flops, bytes_accessed=moved, transcendentals=0)


def constants():
    table = dct()
    eye2, eye4 = np.eye(2), np.eye(4)
    left = two(np.kron(eye2, table))
    right = two(np.kron(eye4, table.T))
    left_back = two(np.kron(eye2, table.T))
    right_back = two(np.kron(eye4, table))
    m = np.arange(LANES)[:, None]
    spread = (m // TOPK == np.arange(256)[None, :] // TILE).astype(ml_dtypes.bfloat16)
    pair = np.kron(eye2, table)
    cross = np.roll(pair, TILE, axis=1)
    decode_right = two(np.concatenate([pair, cross], axis=1))
    decode_left = two(np.concatenate([table[0::2], table[1::2]], axis=0).T)
    return left, right, left_back, right_back, spread, decode_right, decode_left


def own_specs():
    return [
        pl.BlockSpec((1, ROWS, COLS // HALVES), lambda g, rep: (0, 0, g)),
        pl.BlockSpec((1, ROWS, COLS // HALVES), lambda g, rep: (0, 0, g)),
        pl.BlockSpec((1, 2, COLS // HALVES // 2), lambda g, rep: (rep[0], 0, g)),
        whole((2, ROWS, ROWS)),
        whole((2, 256, 256)),
        whole((LANES, 256)),
    ]


def on_device(momentum, grad, weight, indices):
    left, right, left_back, right_back, spread, decode_right, decode_left = constants()
    rep = lax.axis_index("rep").astype(jnp.int32).reshape(1)
    picked = pl.pallas_call(
        pick_kernel,
        out_shape=jax.ShapeDtypeStruct((ZQ * YQ, 2, COLS // 2), jnp.float32),
        grid_spec=pltpu.PrefetchScalarGridSpec(
            num_scalar_prefetch=1,
            grid=(HALVES,),
            in_specs=own_specs() + [whole((256, LANES))],
            out_specs=pl.BlockSpec((ZQ * YQ, 2, COLS // HALVES // 2), lambda g, rep: (0, 0, g)),
            scratch_shapes=[pltpu.VMEM((ROWS * GROUPS // HALVES, 256), jnp.float32)],
        ),
        compiler_params=params(),
        cost_estimate=cost(1 << 30, 3 << 20),
    )(rep, momentum, grad, indices, left, right, spread, spread.T)

    far = lax.all_to_all(picked, "rep", 0, 0, tiled=True, axis_index_groups=far_groups())
    moment_out = pl.pallas_call(
        residual_kernel,
        out_shape=jax.ShapeDtypeStruct(momentum.shape, jnp.float32),
        grid_spec=pltpu.PrefetchScalarGridSpec(
            num_scalar_prefetch=1,
            grid=(HALVES,),
            in_specs=own_specs() + [whole((2, ROWS, ROWS)), whole((2, 256, 256))],
            out_specs=pl.BlockSpec((1, ROWS, COLS // HALVES), lambda g, rep: (0, 0, g)),
            scratch_shapes=[pltpu.VMEM((ROWS * GROUPS // HALVES, 256), jnp.float32)],
        ),
        compiler_params=params(),
        cost_estimate=cost(1 << 31, 5 << 20),
    )(rep, momentum, grad, indices, left, right, spread, left_back, right_back)

    any_space = pl.BlockSpec(memory_space=pl.ANY)
    flat = indices.reshape(N_REP, COLS)
    tables, deeps = [], []
    for first, count in ((0, EARLY), (EARLY, PAIRS - EARLY)):
        table, deep = pl.pallas_call(
            functools.partial(table_kernel, first, count),
            out_shape=(
                jax.ShapeDtypeStruct((count * LANES, LANES), jnp.int32),
                jax.ShapeDtypeStruct((count,), jnp.int32),
            ),
            grid=(1,),
            in_specs=[any_space],
            out_specs=(
                pl.BlockSpec((count * LANES, LANES), lambda s: (0, 0)),
                pl.BlockSpec(memory_space=pltpu.SMEM),
            ),
            scratch_shapes=[
                pltpu.VMEM((N_REP, LANES), jnp.float32),
                pltpu.VMEM((N_REP, count * LANES), jnp.int32),
                pltpu.SemaphoreType.DMA,
            ],
            compiler_params=params(60 << 20),
            cost_estimate=cost(count << 30, 2 << 20),
        )(flat)
        tables.append(table)
        deeps.append(deep)

    far, moment_out, tables[0] = lax.optimization_barrier((far, moment_out, tables[0]))
    near = jnp.broadcast_to(far.reshape(1, ZQ * YQ, COLS), (ZR * YR, ZQ * YQ, COLS))
    every = lax.all_to_all(near, "rep", 0, 0, tiled=True, axis_index_groups=near_groups())
    every = every.reshape(N_REP, COLS)

    summed, energy = pl.pallas_call(
        sum_kernel,
        out_shape=(
            pltpu.HBM((COLS, LANES), jnp.float32),
            jax.ShapeDtypeStruct((N_TP, 8, LANES), jnp.float32),
        ),
        grid_spec=pltpu.PrefetchScalarGridSpec(
            num_scalar_prefetch=2,
            grid=(PAIRS // CHUNK,),
            in_specs=[
                pl.BlockSpec((N_REP, CHUNK * LANES), lambda s, *_: (0, s)),
                pl.BlockSpec((CHUNK * LANES, LANES), lambda s, *_: (jnp.minimum(s, EARLY // CHUNK - 1), 0)),
                pl.BlockSpec((CHUNK * LANES, LANES), lambda s, *_: (jnp.maximum(s - EARLY // CHUNK, 0), 0)),
            ],
            out_specs=(
                pl.BlockSpec((CHUNK * LANES, LANES), lambda s, *_: (s, 0)),
                whole((N_TP, 8, LANES)),
            ),
            scratch_shapes=[pltpu.VMEM((8, LANES), jnp.float32)],
        ),
        compiler_params=params(61341696),
        cost_estimate=cost(6 << 30, 5 << 20),
    )(*deeps, every, *tables)

    energies = lax.all_to_all(energy, "tp", 0, 0, tiled=True)

    decoded = pl.pallas_call(
        decode_kernel,
        out_shape=jax.ShapeDtypeStruct((ROWS, COLS), jnp.float32),
        grid=(2,),
        in_specs=[
            pl.BlockSpec((COLS // 2, LANES), lambda s: (s, 0)),
            whole((2, LANES, 256)),
            whole((2, TILE, TILE)),
        ],
        out_specs=pl.BlockSpec((TILE, COLS), lambda s: (s, 0)),
        scratch_shapes=[pltpu.VMEM((COLS // 2, 256), jnp.float32)],
        compiler_params=params(),
        cost_estimate=cost(1 << 30, 4 << 20),
    )(summed, decode_right, decode_left)

    weight_out = pl.pallas_call(
        update_kernel,
        out_shape=jax.ShapeDtypeStruct((ROWS, COLS), jnp.float32),
        grid=(2,),
        in_specs=[
            pl.BlockSpec((ROWS // 2, COLS), lambda s: (s, 0)),
            pl.BlockSpec((ROWS // 2, COLS), lambda s: (s, 0)),
            whole((N_TP, 8, LANES)),
        ],
        out_specs=pl.BlockSpec((ROWS // 2, COLS), lambda s: (s, 0)),
        compiler_params=params(),
        cost_estimate=cost(1 << 20, 6 << 20),
    )(weight, decoded, energies)
    return moment_out, weight_out


def solution(mesh):
    in_specs = (P("rep", None, "tp"), P("rep", None, "tp"), P(None, "tp"), P(None, None, "tp"))
    out_specs = (P("rep", None, "tp"), P(None, "tp"))
    return jax.shard_map(
        on_device, mesh=mesh, in_specs=in_specs, out_specs=out_specs, check_vma=False
    )
```
